32 devices in a mesh: groups: 2 (over y), tensor: 4 (over z), dp: 4 (over x, core).
Axes of the slice: x: 2, y: 2, z: 4, core: 2. Of those that a mesh axis runs over, the one named last changes fastest.
Arguments:
- hidden_states: bfloat16 [8, 128, 8192], P(('groups', 'dp'), None, 'tensor'), parts along dimension 0, may hold values from -4 to 4
- norm_gain: bfloat16 [8192], P('tensor'), may hold values from 0.5 to 1.5
- w_query: bfloat16 [8192, 8192], P(None, 'tensor'), may hold values from -0.125 to 0.125
- b_query: bfloat16 [8192], P('tensor'), may hold values from -12 to 12
- w_key: bfloat16 [8192, 1024], P(None, 'tensor'), may hold values from -0.0625 to 0.0625
- b_key: bfloat16 [1024], P('tensor'), may hold values from -4 to 4
- w_value: bfloat16 [8192, 1024], P(None, 'tensor'), may hold values from -0.0625 to 0.0625
- b_value: bfloat16 [1024], P('tensor'), may hold values from -4 to 4
- w_out: bfloat16 [8192, 8192], P('tensor'), may hold values from -0.75 to 0.75
- cache_keys: bfloat16 [8, 16384, 1024], P(('groups', 'dp'), 'tensor'), parts along dimension 0, may hold values from -12.5 to 12.5
- cache_values: bfloat16 [8, 16384, 1024], P(('groups', 'dp'), 'tensor'), parts along dimension 0, may hold values from -6 to 6
- cached_lens: int32 [8], P(('groups', 'dp')), parts along dimension 0, may hold values from 4096 to 16384, as said below
- positions: int32 [8, 128], P(('groups', 'dp')), parts along dimension 0, may hold values from 4096 to 16511, as said below
Outputs:
- hidden_out: bfloat16 [8, 128, 8192], P(('groups', 'dp'), None, 'tensor'), parts along dimension 0
The draws below stay inside these ranges and needn't reach their ends.
There are 2 independent parts, one for each index of `groups`. The reference program is written for one: setup_inputs(seed, part) draws one part's arguments, and reference() takes and returns one part's arrays. A program takes and returns all parts, laid end to end along the dimension named above; an argument that names none is the same for every part. Nothing has to cross between parts.
Inputs may be any that keep to these rules, and one draw needn't show every extreme that they name: `cached_lens`: in every part at least one prompt has exactly 16384 cached positions. positions[p, i] = cached_lens[p] + i.
All inputs are finite; a program needn't handle non-finite values.
Results may differ from the reference program's by a relative error of at most 0.013.
Values may be sent and summed in bfloat16 or wider, within the bound.
A program may use at most 448 MiB of HBM per device.

```python
import math
import jax
import jax.numpy as jnp
from jax import lax

D = 8192
H = 64
KVH = 8
HD = 128
QB = 128
TOK = 128
CACHE = 16384
PROMPTS = 4
QHEADS_DEV = 16
CACHE_BLOCK = 4096
NEW_BLOCK = 32


def shared_lengths(key):
    key_len, key_pick = jax.random.split(key)
    drawn = jax.random.randint(key_len, (PROMPTS,), CACHE // 4, CACHE + 1)
    chosen = jax.random.randint(key_pick, (), 0, PROMPTS)
    return jnp.where(jnp.arange(PROMPTS) == chosen, CACHE, drawn).astype(jnp.int32)


def draw_cached_lens(key, part):
    return shared_lengths(key)


def draw_positions(key, part):
    lengths = shared_lengths(key)
    return (lengths[:, None] + jnp.arange(TOK, dtype=jnp.int32)[None, :]).astype(jnp.int32)


def draw_hidden_states(key, part):
    key = jax.random.fold_in(key, 3)
    key_row, key_col, key_base = jax.random.split(key, 3)
    feature = jnp.arange(D, dtype=jnp.float32) / D
    spread = math.log(10.0)
    rising = jnp.exp(math.log(3.0) * (feature - 1.0))
    row_scale = jnp.exp(jax.random.uniform(key_row, (PROMPTS, TOK, 1), minval=-spread, maxval=0.0))
    col_scale = jnp.exp(jax.random.uniform(key_col, (1, 1, D), minval=-spread, maxval=0.0)) * rising
    base_values = jax.random.truncated_normal(key_base, -4.0, 4.0, (PROMPTS, TOK, D))
    return (row_scale * col_scale * base_values).astype(jnp.bfloat16)


def draw_b_query(key, part):
    key = jax.random.fold_in(key, 5)
    key_noise = jax.random.fold_in(key, 0)
    return jax.random.truncated_normal(key_noise, -4.0, 4.0, (H * HD,)).astype(jnp.bfloat16)


def draw_cache_keys(key, part):
    key = jax.random.fold_in(key, 7)
    key_base = jax.random.fold_in(key, 0)
    return jax.random.truncated_normal(key_base, -6.0, 6.0, (PROMPTS, CACHE, KVH * HD)).astype(jnp.bfloat16)


def shard_levels(key, shape, shards, smallest, high):
    level = 1.0
    for dim, parts in shards:
        heights = jax.random.uniform(jax.random.fold_in(jax.random.fold_in(key, 6), dim), (parts,), jnp.float32, smallest / len(shards), high / len(shards))
        level = level * jnp.repeat(jnp.exp(heights), shape[dim] // parts).reshape((-1,) + (1,) * (len(shape) - 1 - dim))
    return level


def scatter_about(own_key, extent, width, reach, pieces=(), kind=jnp.bfloat16):
    entries = width * jax.random.normal(own_key, extent, jnp.float32)
    if pieces:
        entries = entries * shard_levels(own_key, extent, pieces, -0.22, 0.18)
    return jnp.clip(entries, -reach, reach).astype(kind)


def setup_inputs(seed: int = 0, part: int = 0) -> dict:
    key_of = jax.random.split(jax.random.key(seed), 14)
    part_splits = jax.random.split(jax.random.fold_in(key_of[13], part), 14)
    return {
        "hidden_states": draw_hidden_states(jax.random.fold_in(jax.random.fold_in(key_of[13], part), 71), part),
        "norm_gain": jnp.clip(1.0 + 0.1 * jax.random.normal(key_of[1], (D,), jnp.float32), 0.5, 1.5).astype(jnp.bfloat16),
        "w_query": scatter_about(key_of[2], (D, H * HD), (D // 4) ** -0.5, 0.125, ((1, 4),)),
        "b_query": draw_b_query(jax.random.fold_in(key_of[13], 71), part),
        "w_key": scatter_about(key_of[4], (D, KVH * HD), D ** -0.5, 0.0625, ((1, 4),)),
        "b_key": scatter_about(key_of[5], (KVH * HD,), 1.0, 4.0, ((0, 4),)),
        "w_value": scatter_about(key_of[6], (D, KVH * HD), D ** -0.5, 0.0625, ((1, 4),)),
        "b_value": scatter_about(key_of[7], (KVH * HD,), 1.0, 4.0, ((0, 4),)),
        "w_out": scatter_about(key_of[8], (H * HD, D), (HD // 2) ** -0.5, 0.75, ((0, 4),)),
        "cache_keys": draw_cache_keys(jax.random.fold_in(jax.random.fold_in(key_of[13], part), 71), part),
        "cache_values": scatter_about(part_splits[10], (PROMPTS, CACHE, KVH * HD), 1.0, 6.0, ((0, 4), (1, 4))),
        "cached_lens": draw_cached_lens(jax.random.fold_in(jax.random.fold_in(key_of[13], part), 71), part),
        "positions": draw_positions(jax.random.fold_in(jax.random.fold_in(key_of[13], part), 71), part),
    }


ROPE_BASE = 1000000.0
NORM_EPS = 1e-06
MASK_FILL = -1e+30

def quantize(values):
    biggest = lax.optimization_barrier(jnp.max(jnp.abs(values), axis=-1))
    block_scale = ((biggest + 1e-06) / 127.0).astype(jnp.bfloat16)
    payload = (values / block_scale.astype(jnp.float32)[..., None]).astype(jnp.bfloat16)
    return (payload, block_scale)

def dequantize(payload, block_scale):
    return payload.astype(jnp.float32) * block_scale.astype(jnp.float32)[..., None]

def rotate_cols(values, token_pos, first_col):
    row_count = values.shape[0]
    pair_count = values.shape[1] // 2
    column = first_col + 2 * jnp.arange(pair_count, dtype=jnp.int32)
    pair_index = column % HD // 2
    inverse = jnp.power(ROPE_BASE, -2.0 * pair_index.astype(jnp.float32) / HD)
    angles = token_pos.astype(jnp.float32)[:, None] * inverse[None, :]
    cosine = jnp.cos(angles)
    sine_part = jnp.sin(angles)
    paired = values.reshape(row_count, pair_count, 2)
    even_part = paired[:, :, 0]
    odd_part = paired[:, :, 1]
    turned = jnp.stack([even_part * cosine - odd_part * sine_part, odd_part * cosine + even_part * sine_part], axis=-1)
    return turned.reshape(row_count, pair_count * 2)

def block_terms(queries, keys_all, values_all, allowed):
    scores = jnp.einsum('tgqd,lgd->tgql', queries, keys_all) / math.sqrt(HD)
    visible = allowed[:, None, None, :]
    masked = jnp.where(visible, scores, MASK_FILL)
    block_max = lax.optimization_barrier(jnp.max(masked, axis=-1))
    exp_terms = jnp.where(visible, jnp.exp(masked - block_max[..., None]), 0.0)
    block_total = lax.optimization_barrier(jnp.sum(exp_terms, axis=-1))
    weights = exp_terms.astype(jnp.bfloat16).astype(jnp.float32)
    summed = jnp.einsum('tgql,lgd->tgqd', weights, values_all)
    return (block_max, block_total, summed)

def reference(hidden_states, norm_gain, w_query, b_query, w_key, b_key, w_value, b_value, w_out, cache_keys, cache_values, cached_lens, positions):
    row_count = PROMPTS * TOK
    block_count = D // QB
    payload, block_scale = quantize(hidden_states.astype(jnp.float32).reshape(row_count, block_count, QB))
    restored = dequantize(payload, block_scale)
    inv_rms = lax.rsqrt(lax.optimization_barrier(jnp.sum(restored * restored, axis=(1, 2))) / D + NORM_EPS)
    scaled = (restored * norm_gain.astype(jnp.float32).reshape(1, block_count, QB)).astype(jnp.bfloat16).reshape(row_count, D)
    row_scale = inv_rms[:, None]
    token_pos = positions.reshape(row_count)
    query_full = row_scale * jnp.dot(scaled, w_query, preferred_element_type=jnp.float32) + b_query.astype(jnp.float32)
    key_full = row_scale * jnp.dot(scaled, w_key, preferred_element_type=jnp.float32) + b_key.astype(jnp.float32)
    value_new = (row_scale * jnp.dot(scaled, w_value, preferred_element_type=jnp.float32) + b_value.astype(jnp.float32)).astype(jnp.bfloat16)
    query_rot = rotate_cols(query_full, token_pos, 0).astype(jnp.bfloat16)
    key_rot = rotate_cols(key_full, token_pos, 0).astype(jnp.bfloat16)
    group_size = H // KVH
    key_blocks = CACHE // CACHE_BLOCK
    attended_list = []
    for prompt in range(PROMPTS):
        queries = query_rot[prompt * TOK:(prompt + 1) * TOK].astype(jnp.float32).reshape(TOK, KVH, group_size, HD)
        fresh_keys = key_rot[prompt * TOK:(prompt + 1) * TOK].astype(jnp.float32).reshape(TOK, KVH, HD)
        fresh_values = value_new[prompt * TOK:(prompt + 1) * TOK].astype(jnp.float32).reshape(TOK, KVH, HD)
        length = cached_lens[prompt]
        prompt_keys = cache_keys[prompt]
        prompt_values = cache_values[prompt]

        def one_block(state_in, block_id):
            run_max, run_num, run_den = state_in
            cache_part = lax.dynamic_slice_in_dim(prompt_keys, block_id * CACHE_BLOCK, CACHE_BLOCK, 0).astype(jnp.float32).reshape(CACHE_BLOCK, KVH, HD)
            cache_vals = lax.dynamic_slice_in_dim(prompt_values, block_id * CACHE_BLOCK, CACHE_BLOCK, 0).astype(jnp.float32).reshape(CACHE_BLOCK, KVH, HD)
            new_part = lax.dynamic_slice_in_dim(fresh_keys, block_id * NEW_BLOCK, NEW_BLOCK, 0)
            new_vals = lax.dynamic_slice_in_dim(fresh_values, block_id * NEW_BLOCK, NEW_BLOCK, 0)
            keys_all = jnp.concatenate([cache_part, new_part], axis=0)
            values_all = jnp.concatenate([cache_vals, new_vals], axis=0)
            cache_pos = block_id * CACHE_BLOCK + jnp.arange(CACHE_BLOCK, dtype=jnp.int32)
            new_pos = block_id * NEW_BLOCK + jnp.arange(NEW_BLOCK, dtype=jnp.int32)
            token_ids = jnp.arange(TOK, dtype=jnp.int32)
            allowed = jnp.concatenate([jnp.broadcast_to((cache_pos < length)[None, :], (TOK, CACHE_BLOCK)), new_pos[None, :] <= token_ids[:, None]], axis=1)
            block_max, block_total, summed = block_terms(queries, keys_all, values_all, allowed)
            new_max = jnp.maximum(run_max, block_max)
            old_factor = jnp.exp(run_max - new_max)
            new_factor = jnp.exp(block_max - new_max)
            run_num = run_num * old_factor[..., None] + summed * new_factor[..., None]
            run_den = run_den * old_factor + block_total * new_factor
            return ((new_max, run_num, run_den), None)
        start_state = (jnp.full((TOK, KVH, group_size), MASK_FILL, jnp.float32), jnp.zeros((TOK, KVH, group_size, HD), jnp.float32), jnp.zeros((TOK, KVH, group_size), jnp.float32))
        final_state, _ = lax.scan(one_block, start_state, jnp.arange(key_blocks, dtype=jnp.int32))
        attended_list.append((final_state[1] / final_state[2][..., None]).astype(jnp.bfloat16).reshape(TOK, H * HD))
    attended = jnp.concatenate(attended_list, axis=0)
    head_cols = QHEADS_DEV * HD

    def project(running, block_id):
        columns = lax.dynamic_slice_in_dim(attended, block_id * head_cols, head_cols, 1)
        weight_rows = lax.dynamic_slice_in_dim(w_out, block_id * head_cols, head_cols, 0)
        projected = jnp.dot(columns, weight_rows, preferred_element_type=jnp.float32).reshape(row_count, block_count, QB)
        out_pay, out_scale = quantize(projected)
        return (running + dequantize(out_pay, out_scale), None)
    running_sum, _ = lax.scan(project, jnp.zeros((row_count, block_count, QB), jnp.float32), jnp.arange(H // QHEADS_DEV, dtype=jnp.int32))
    result = hidden_states.astype(jnp.float32).reshape(row_count, block_count, QB) + running_sum
    return result.astype(jnp.bfloat16).reshape(PROMPTS, TOK, D)
```

```python
import functools
import math

import jax
import jax.numpy as jnp
from jax import lax
from jax.experimental import pallas as pl
from jax.experimental.pallas import tpu as pltpu
from jax.sharding import PartitionSpec as P

HD = 128
QB = 128


ROPE_BASE = 1000000.0
NORM_EPS = 1e-06
MASK_FILL = -1e30
LOG2E = 1.4426950408889634
TILE_ROWS = 256


def quantize(values):
    biggest = jnp.max(jnp.abs(values), axis=-1)
    block_scale = ((biggest + 1e-06) / 127.0).astype(jnp.bfloat16)
    payload = (values / block_scale.astype(jnp.float32)[..., None]).astype(jnp.bfloat16)
    return (payload, block_scale)


def dequantize(payload, block_scale):
    return payload.astype(jnp.float32) * block_scale.astype(jnp.float32)[..., None]


def rotation_tables(token_pos):
    column = jnp.arange(HD, dtype=jnp.int32)
    pair_index = column // 2
    inverse = jnp.power(ROPE_BASE, -2.0 * pair_index.astype(jnp.float32) / HD)
    angles = token_pos.astype(jnp.float32)[:, None] * inverse[None, :]
    sign = jnp.where(column % 2 == 0, -1.0, 1.0)
    return jnp.cos(angles), jnp.sin(angles) * sign[None, :]


def fit_table(table, first_col, cols):
    if cols >= HD:
        return jnp.tile(table, (1, cols // HD))
    return lax.dynamic_slice_in_dim(table, first_col % HD, cols, 1)


def rotate_cols(values, cosine, sine):
    even = jnp.arange(values.shape[1], dtype=jnp.int32) % 2 == 0
    swapped = jnp.where(even[None, :], jnp.roll(values, -1, axis=1), jnp.roll(values, 1, axis=1))
    return values * cosine + swapped * sine


def attend_kernel(group, cache_tile, info, q_ref, k_ref, v_ref, nk_ref, nv_ref, acc_ref, stat_ref, s0, s1):
    head = pl.program_id(0)
    tokens = q_ref.shape[0]
    cache_count = k_ref.shape[0]
    new_count = nk_ref.shape[0]
    heads_tile = TILE_ROWS // tokens
    tiles = group // heads_tile
    head_count = group * pl.num_programs(0)
    scratch = (s0, s1)
    visible, new_first, new_valid = info[0], info[1], info[2]
    spans = [(lo, min(cache_tile, cache_count - lo)) for lo in range(0, cache_count, cache_tile)]
    nt = (((1,), (1,)), ((), ()))

    def score(tile, buffer):
        queries = jnp.concatenate(
            [q_ref[:, pl.ds((tile * heads_tile + j) * HD, HD)] for j in range(heads_tile)], axis=0
        )
        best = jnp.full((TILE_ROWS, 128), MASK_FILL, jnp.float32)
        for lo, size in spans:
            raw = lax.dot_general(queries, k_ref[pl.ds(lo, size), :], nt, preferred_element_type=jnp.float32)
            place = lo + lax.broadcasted_iota(jnp.int32, (1, size), 1)
            raw = jnp.where(place < visible, raw, MASK_FILL)
            buffer[:, pl.ds(lo, size)] = raw
            for c in range(0, size, 128):
                best = jnp.maximum(best, raw[:, c : c + 128])
        raw = lax.dot_general(queries, nk_ref[...], nt, preferred_element_type=jnp.float32)
        place = lax.broadcasted_iota(jnp.int32, (TILE_ROWS, new_count), 1)
        token = lax.broadcasted_iota(jnp.int32, (TILE_ROWS, new_count), 0) % tokens
        raw = jnp.where((place < new_valid) & (new_first + place <= token), raw, MASK_FILL)
        buffer[:, pl.ds(cache_count, new_count)] = raw
        for c in range(0, new_count, 128):
            best = jnp.maximum(best, raw[:, c : c + 128])
        return jnp.max(best, axis=1, keepdims=True)

    lane = lax.broadcasted_iota(jnp.int32, (tokens, stat_ref.shape[1]), 1)

    def weigh(tile, buffer, top):
        shift = jnp.where(top > 0.5 * MASK_FILL, top, 0.0)
        total = jnp.zeros((TILE_ROWS, 2 * HD), jnp.float32)
        for lo, size in spans + [(cache_count, new_count)]:
            weight = jnp.exp2(buffer[:, pl.ds(lo, size)] - shift).astype(jnp.bfloat16)
            value = v_ref[pl.ds(lo, size), :] if lo < cache_count else nv_ref[...]
            value = jnp.concatenate([value, jnp.ones((size, HD), jnp.bfloat16)], axis=1)
            total += jnp.dot(weight, value, preferred_element_type=jnp.float32)
        for j in range(heads_tile):
            index = tile * heads_tile + j
            rows = slice(j * tokens, (j + 1) * tokens)
            acc_ref[:, pl.ds(index * HD, HD)] = total[rows, :HD].astype(jnp.bfloat16)
            where = head * group + index
            stats = jnp.where(lane == where, jnp.broadcast_to(top[rows], lane.shape), stat_ref[...])
            stat_ref[...] = jnp.where(lane == head_count + where, total[rows, HD : HD + 1], stats)

    @pl.when(head == 0)
    def _():
        stat_ref[...] = jnp.zeros_like(stat_ref)

    top = score(0, scratch[0])
    for tile in range(tiles):
        later = score(tile + 1, scratch[(tile + 1) % 2]) if tile + 1 < tiles else None
        weigh(tile, scratch[tile % 2], top)
        top = later


def attend(queries, cache_k, cache_v, new_k, new_v, info, kv_heads):
    tokens, width = queries.shape
    group = width // HD // kv_heads
    cache_count = cache_k.shape[0]
    new_count = new_k.shape[0]
    return pl.pallas_call(
        functools.partial(attend_kernel, group, min(1024, cache_count)),
        grid=(kv_heads,),
        in_specs=[
            pl.BlockSpec(memory_space=pltpu.SMEM),
            pl.BlockSpec((tokens, group * HD), lambda g: (0, g)),
            pl.BlockSpec((cache_count, HD), lambda g: (0, g)),
            pl.BlockSpec((cache_count, HD), lambda g: (0, g)),
            pl.BlockSpec((new_count, HD), lambda g: (0, g)),
            pl.BlockSpec((new_count, HD), lambda g: (0, g)),
        ],
        out_specs=[
            pl.BlockSpec((tokens, group * HD), lambda g: (0, g)),
            pl.BlockSpec((tokens, 2 * width // HD), lambda g: (0, 0)),
        ],
        out_shape=[
            jax.ShapeDtypeStruct((tokens, width), jnp.bfloat16),
            jax.ShapeDtypeStruct((tokens, 2 * width // HD), jnp.float32),
        ],
        scratch_shapes=[pltpu.VMEM((TILE_ROWS, cache_count + new_count), jnp.float32)] * 2,
        compiler_params=pltpu.CompilerParams(vmem_limit_bytes=48 * 1024 * 1024),
        cost_estimate=pl.CostEstimate(
            flops=4 * tokens * width * (cache_count + new_count),
            bytes_accessed=4 * cache_count * kv_heads * HD + 4 * tokens * width,
            transcendentals=tokens * width // HD * (cache_count + new_count),
        ),
    )(info, queries, cache_k, cache_v, new_k, new_v)


def on_device(
    hidden_states,
    norm_gain,
    w_query,
    b_query,
    w_key,
    b_key,
    w_value,
    b_value,
    w_out,
    cache_keys,
    cache_values,
    cached_lens,
    positions,
):
    devices = lax.axis_size("tensor")
    tensor_rank = lax.axis_index("tensor")
    tokens = hidden_states.shape[1]
    feat_dev = hidden_states.shape[2]
    blocks_dev = feat_dev // QB
    full_width = feat_dev * devices
    query_cols = w_query.shape[1]
    kv_cols = w_key.shape[1]
    local_rows = hidden_states[0].astype(jnp.float32)
    payload, block_scale = quantize(local_rows.reshape(tokens, blocks_dev, QB))
    restored = dequantize(payload, block_scale)
    gain_rows = norm_gain.reshape(1, blocks_dev, QB).astype(jnp.float32)
    scaled_dev = (restored * gain_rows).astype(jnp.bfloat16).reshape(tokens, feat_dev)
    squares = lax.psum(jnp.sum(restored * restored, axis=(1, 2)), "tensor")
    scaled = lax.all_gather(scaled_dev, "tensor", axis=1, tiled=True)
    query_acc = jnp.dot(scaled, w_query, preferred_element_type=jnp.float32)
    key_acc = jnp.dot(scaled, w_key, preferred_element_type=jnp.float32)
    value_acc = jnp.dot(scaled, w_value, preferred_element_type=jnp.float32)
    inv_rms = lax.rsqrt(squares / full_width + NORM_EPS)
    row_scale = inv_rms[:, None]
    cosine, sine = rotation_tables(positions[0])
    query_full = row_scale * query_acc + b_query.astype(jnp.float32)
    key_full = row_scale * key_acc + b_key.astype(jnp.float32)
    fold = LOG2E / math.sqrt(HD)
    query_rot = rotate_cols(
        query_full,
        fit_table(cosine * fold, tensor_rank * query_cols, query_cols),
        fit_table(sine * fold, tensor_rank * query_cols, query_cols),
    ).astype(jnp.bfloat16)
    key_rot = rotate_cols(
        key_full,
        fit_table(cosine, tensor_rank * kv_cols, kv_cols),
        fit_table(sine, tensor_rank * kv_cols, kv_cols),
    ).astype(jnp.bfloat16)
    value_new = (row_scale * value_acc + b_value.astype(jnp.float32)).astype(jnp.bfloat16)
    cache_count = cache_keys.shape[1]
    per_dev = query_cols // HD
    block_keys, block_values = (
        lax.all_to_all(key_rot, "tensor", split_axis=0, concat_axis=1, tiled=True),
        lax.all_to_all(value_new, "tensor", split_axis=0, concat_axis=1, tiled=True),
    )
    all_queries = lax.all_gather(query_rot, "tensor", axis=1, tiled=True)
    kv_heads = block_keys.shape[1] // HD
    new_count = block_keys.shape[0]
    pad = -new_count % 128
    info = jnp.stack(
        [cached_lens[0] - tensor_rank * cache_count, tensor_rank * new_count, jnp.int32(new_count)]
    ).astype(jnp.int32)
    sums, stats = attend(
        all_queries,
        cache_keys[0],
        cache_values[0],
        jnp.pad(block_keys, ((0, pad), (0, 0))),
        jnp.pad(block_values, ((0, pad), (0, 0))),
        info,
        kv_heads,
    )
    acc_in = lax.all_to_all(
        sums.reshape(tokens, devices, per_dev * HD), "tensor", split_axis=1, concat_axis=1, tiled=True
    )
    stat_in = lax.all_to_all(
        stats.reshape(tokens, 2, devices, per_dev), "tensor", split_axis=2, concat_axis=2, tiled=True
    )
    max_in, tot_in = stat_in[:, 0], stat_in[:, 1]
    top_max = jnp.max(max_in, axis=1, keepdims=True)
    factor = jnp.exp2(max_in - top_max)
    numerator = jnp.sum(
        acc_in.astype(jnp.float32).reshape(tokens, devices, per_dev, HD) * factor[..., None], axis=1
    )
    denominator = jnp.sum(factor * tot_in, axis=1)
    attended = (
        (numerator / denominator[..., None]).astype(jnp.bfloat16).reshape(tokens, per_dev * HD)
    )
    projected = jnp.dot(attended, w_out, preferred_element_type=jnp.float32)
    out_pay, out_scale = quantize(projected.reshape(tokens, full_width // QB, QB))
    recv_pay, recv_scale = (
        lax.all_to_all(out_pay, "tensor", split_axis=1, concat_axis=0, tiled=True),
        lax.all_to_all(out_scale, "tensor", split_axis=1, concat_axis=0, tiled=True),
    )
    summed_in = jnp.sum(
        dequantize(recv_pay, recv_scale).reshape(devices, tokens, blocks_dev, QB), axis=0
    )
    result = (local_rows + summed_in.reshape(tokens, feat_dev)).astype(jnp.bfloat16)
    return result[None]


def solution(mesh):
    return jax.shard_map(
        on_device,
        mesh=mesh,
        in_specs=(
            P(("groups", "dp"), None, "tensor"),
            P("tensor"),
            P(None, "tensor"),
            P("tensor"),
            P(None, "tensor"),
            P("tensor"),
            P(None, "tensor"),
            P("tensor"),
            P("tensor", None),
            P(("groups", "dp"), "tensor", None),
            P(("groups", "dp"), "tensor", None),
            P(("groups", "dp")),
            P(("groups", "dp"), None),
        ),
        out_specs=P(("groups", "dp"), None, "tensor"),
        check_vma=False,
    )
```

```python
import functools
import math

import jax
import jax.numpy as jnp
from jax import lax
from jax.experimental import pallas as pl
from jax.experimental.pallas import tpu as pltpu
from jax.sharding import PartitionSpec as P

HD = 128
QB = 128


ROPE_BASE = 1000000.0
NORM_EPS = 1e-06
MASK_FILL = -1e30
LOG2E = 1.4426950408889634
TILE_ROWS = 256


def quantize(values):
    biggest = jnp.max(jnp.abs(values), axis=-1)
    block_scale = ((biggest + 1e-06) / 127.0).astype(jnp.bfloat16)
    payload = (values / block_scale.astype(jnp.float32)[..., None]).astype(jnp.bfloat16)
    return (payload, block_scale)


def dequantize(payload, block_scale):
    return payload.astype(jnp.float32) * block_scale.astype(jnp.float32)[..., None]


def rotation_tables(token_pos):
    column = jnp.arange(HD, dtype=jnp.int32)
    pair_index = column // 2
    inverse = jnp.power(ROPE_BASE, -2.0 * pair_index.astype(jnp.float32) / HD)
    angles = token_pos.astype(jnp.float32)[:, None] * inverse[None, :]
    sign = jnp.where(column % 2 == 0, -1.0, 1.0)
    return jnp.cos(angles), jnp.sin(angles) * sign[None, :]


def fit_table(table, first_col, cols):
    if cols >= HD:
        return jnp.tile(table, (1, cols // HD))
    return lax.dynamic_slice_in_dim(table, first_col % HD, cols, 1)


def rotate_cols(values, cosine, sine):
    even = jnp.arange(values.shape[1], dtype=jnp.int32) % 2 == 0
    swapped = jnp.where(even[None, :], jnp.roll(values, -1, axis=1), jnp.roll(values, 1, axis=1))
    return values * cosine + swapped * sine


def attend_kernel(group, cache_tile, info, q_ref, k_ref, v_ref, nk_ref, nv_ref, acc_ref, stat_ref, s0, s1):
    head = pl.program_id(0)
    tokens = q_ref.shape[0]
    cache_count = k_ref.shape[0]
    new_count = nk_ref.shape[0]
    heads_tile = TILE_ROWS // tokens
    tiles = group // heads_tile
    head_count = group * pl.num_programs(0)
    scratch = (s0, s1)
    visible, new_first, new_valid = info[0], info[1], info[2]
    spans = [(lo, min(cache_tile, cache_count - lo)) for lo in range(0, cache_count, cache_tile)]
    nt = (((1,), (1,)), ((), ()))

    def score(tile, buffer):
        queries = jnp.concatenate(
            [q_ref[:, pl.ds((tile * heads_tile + j) * HD, HD)] for j in range(heads_tile)], axis=0
        )
        best = jnp.full((TILE_ROWS, 128), MASK_FILL, jnp.float32)
        for lo, size in spans:
            raw = lax.dot_general(queries, k_ref[pl.ds(lo, size), :], nt, preferred_element_type=jnp.float32)
            place = lo + lax.broadcasted_iota(jnp.int32, (1, size), 1)
            raw = jnp.where(place < visible, raw, MASK_FILL)
            buffer[:, pl.ds(lo, size)] = raw
            for c in range(0, size, 128):
                best = jnp.maximum(best, raw[:, c : c + 128])
        raw = lax.dot_general(queries, nk_ref[...], nt, preferred_element_type=jnp.float32)
        place = lax.broadcasted_iota(jnp.int32, (TILE_ROWS, new_count), 1)
        token = lax.broadcasted_iota(jnp.int32, (TILE_ROWS, new_count), 0) % tokens
        raw = jnp.where((place < new_valid) & (new_first + place <= token), raw, MASK_FILL)
        buffer[:, pl.ds(cache_count, new_count)] = raw
        for c in range(0, new_count, 128):
            best = jnp.maximum(best, raw[:, c : c + 128])
        return jnp.max(best, axis=1, keepdims=True)

    lane = lax.broadcasted_iota(jnp.int32, (tokens, stat_ref.shape[1]), 1)

    def weigh(tile, buffer, top):
        shift = jnp.where(top > 0.5 * MASK_FILL, top, 0.0)
        total = jnp.zeros((TILE_ROWS, 2 * HD), jnp.float32)
        for lo, size in spans + [(cache_count, new_count)]:
            weight = jnp.exp2(buffer[:, pl.ds(lo, size)] - shift).astype(jnp.bfloat16)
            value = v_ref[pl.ds(lo, size), :] if lo < cache_count else nv_ref[...]
            value = jnp.concatenate([value, jnp.ones((size, HD), jnp.bfloat16)], axis=1)
            total += jnp.dot(weight, value, preferred_element_type=jnp.float32)
        for j in range(heads_tile):
            index = tile * heads_tile + j
            rows = slice(j * tokens, (j + 1) * tokens)
            acc_ref[:, pl.ds(index * HD, HD)] = total[rows, :HD].astype(jnp.bfloat16)
            where = head * group + index
            stats = jnp.where(lane == where, jnp.broadcast_to(top[rows], lane.shape), stat_ref[...])
            stat_ref[...] = jnp.where(lane == head_count + where, total[rows, HD : HD + 1], stats)

    @pl.when(head == 0)
    def _():
        stat_ref[...] = jnp.zeros_like(stat_ref)

    top = score(0, scratch[0])
    for tile in range(tiles):
        later = score(tile + 1, scratch[(tile + 1) % 2]) if tile + 1 < tiles else None
        weigh(tile, scratch[tile % 2], top)
        top = later


def attend(queries, cache_k, cache_v, new_k, new_v, info, kv_heads):
    tokens, width = queries.shape
    group = width // HD // kv_heads
    cache_count = cache_k.shape[0]
    new_count = new_k.shape[0]
    return pl.pallas_call(
        functools.partial(attend_kernel, group, min(1024, cache_count)),
        grid=(kv_heads,),
        in_specs=[
            pl.BlockSpec(memory_space=pltpu.SMEM),
            pl.BlockSpec((tokens, group * HD), lambda g: (0, g)),
            pl.BlockSpec((cache_count, HD), lambda g: (0, g)),
            pl.BlockSpec((cache_count, HD), lambda g: (0, g)),
            pl.BlockSpec((new_count, HD), lambda g: (0, g)),
            pl.BlockSpec((new_count, HD), lambda g: (0, g)),
        ],
        out_specs=[
            pl.BlockSpec((tokens, group * HD), lambda g: (0, g)),
            pl.BlockSpec((tokens, 2 * width // HD), lambda g: (0, 0)),
        ],
        out_shape=[
            jax.ShapeDtypeStruct((tokens, width), jnp.bfloat16),
            jax.ShapeDtypeStruct((tokens, 2 * width // HD), jnp.float32),
        ],
        scratch_shapes=[pltpu.VMEM((TILE_ROWS, cache_count + new_count), jnp.float32)] * 2,
        compiler_params=pltpu.CompilerParams(vmem_limit_bytes=48 * 1024 * 1024),
        cost_estimate=pl.CostEstimate(
            flops=4 * tokens * width * (cache_count + new_count),
            bytes_accessed=4 * cache_count * kv_heads * HD + 4 * tokens * width,
            transcendentals=tokens * width // HD * (cache_count + new_count),
        ),
    )(info, queries, cache_k, cache_v, new_k, new_v)


def on_device_split_heads(
    hidden_states,
    norm_gain,
    w_query,
    b_query,
    w_key,
    b_key,
    w_value,
    b_value,
    w_out,
    cache_keys,
    cache_values,
    cached_lens,
    positions,
):
    devices = lax.axis_size("tensor")
    tensor_rank = lax.axis_index("tensor")
    tokens = hidden_states.shape[1]
    feat_dev = hidden_states.shape[2]
    blocks_dev = feat_dev // QB
    full_width = feat_dev * devices
    query_cols = w_query.shape[1]
    kv_cols = w_key.shape[1]
    local_rows = hidden_states[0].astype(jnp.float32)
    payload, block_scale = quantize(local_rows.reshape(tokens, blocks_dev, QB))
    restored = dequantize(payload, block_scale)
    gain_rows = norm_gain.reshape(1, blocks_dev, QB).astype(jnp.float32)
    scaled_dev = (restored * gain_rows).astype(jnp.bfloat16).reshape(tokens, feat_dev)
    squares = lax.psum(jnp.sum(restored * restored, axis=(1, 2)), "tensor")
    scaled = lax.all_gather(scaled_dev, "tensor", axis=1, tiled=True)
    query_acc = jnp.dot(scaled, w_query, preferred_element_type=jnp.float32)
    key_acc = jnp.dot(scaled, w_key, preferred_element_type=jnp.float32)
    value_acc = jnp.dot(scaled, w_value, preferred_element_type=jnp.float32)
    inv_rms = lax.rsqrt(squares / full_width + NORM_EPS)
    row_scale = inv_rms[:, None]
    cosine, sine = rotation_tables(positions[0])
    query_full = row_scale * query_acc + b_query.astype(jnp.float32)
    key_full = row_scale * key_acc + b_key.astype(jnp.float32)
    fold = LOG2E / math.sqrt(HD)
    query_rot = rotate_cols(
        query_full,
        fit_table(cosine * fold, tensor_rank * query_cols, query_cols),
        fit_table(sine * fold, tensor_rank * query_cols, query_cols),
    ).astype(jnp.bfloat16)
    key_rot = rotate_cols(
        key_full,
        fit_table(cosine, tensor_rank * kv_cols, kv_cols),
        fit_table(sine, tensor_rank * kv_cols, kv_cols),
    ).astype(jnp.bfloat16)
    value_new = (row_scale * value_acc + b_value.astype(jnp.float32)).astype(jnp.bfloat16)
    cache_count = cache_keys.shape[1]
    per_dev = query_cols // HD
    block_keys, block_values = (
        lax.all_to_all(key_rot, "tensor", split_axis=0, concat_axis=1, tiled=True),
        lax.all_to_all(value_new, "tensor", split_axis=0, concat_axis=1, tiled=True),
    )
    all_queries = lax.all_gather(query_rot, "tensor", axis=1, tiled=True)
    kv_heads = block_keys.shape[1] // HD
    new_count = block_keys.shape[0]
    pad = -new_count % 128
    info = jnp.stack(
        [cached_lens[0] - tensor_rank * cache_count, tensor_rank * new_count, jnp.int32(new_count)]
    ).astype(jnp.int32)
    sums, stats = attend(
        all_queries,
        cache_keys[0],
        cache_values[0],
        jnp.pad(block_keys, ((0, pad), (0, 0))),
        jnp.pad(block_values, ((0, pad), (0, 0))),
        info,
        kv_heads,
    )
    acc_in = lax.all_to_all(
        sums.reshape(tokens, devices, per_dev * HD), "tensor", split_axis=1, concat_axis=1, tiled=True
    )
    stat_in = lax.all_to_all(
        stats.reshape(tokens, 2, devices, per_dev), "tensor", split_axis=2, concat_axis=2, tiled=True
    )
    max_in, tot_in = stat_in[:, 0], stat_in[:, 1]
    top_max = jnp.max(max_in, axis=1, keepdims=True)
    factor = jnp.exp2(max_in - top_max)
    numerator = jnp.sum(
        acc_in.astype(jnp.float32).reshape(tokens, devices, per_dev, HD) * factor[..., None], axis=1
    )
    denominator = jnp.sum(factor * tot_in, axis=1)
    attended = (
        (numerator / denominator[..., None]).astype(jnp.bfloat16).reshape(tokens, per_dev * HD)
    )
    projected = jnp.dot(attended, w_out, preferred_element_type=jnp.float32)
    out_pay, out_scale = quantize(projected.reshape(tokens, full_width // QB, QB))
    recv_pay, recv_scale = (
        lax.all_to_all(out_pay, "tensor", split_axis=1, concat_axis=0, tiled=True),
        lax.all_to_all(out_scale, "tensor", split_axis=1, concat_axis=0, tiled=True),
    )
    summed_in = jnp.sum(
        dequantize(recv_pay, recv_scale).reshape(devices, tokens, blocks_dev, QB), axis=0
    )
    result = (local_rows + summed_in.reshape(tokens, feat_dev)).astype(jnp.bfloat16)
    return result[None]


def project_kernel(start, x_ref, wq_ref, wk_ref, wv_ref, *rest):
    carried, (q_out, k_out, v_out) = rest[:-3], rest[-3:]
    rows = x_ref[...]

    def step(weight, place):
        term = jnp.dot(rows, weight[...], preferred_element_type=jnp.float32)
        return term + carried[place][...] if carried else term

    q_out[...] = step(wq_ref, 0)

    @pl.when(pl.program_id(0) == 0)
    def _():
        k_out[...] = step(wk_ref, 1)
        v_out[...] = step(wv_ref, 2)


def project_part(origin, rows, w_query, w_key, w_value, carried):
    tokens, depth = rows.shape
    query_cols, kv_cols = w_query.shape[1], w_key.shape[1]
    tile = min(512, query_cols)
    q_spec = pl.BlockSpec((tokens, tile), lambda i, s: (0, i))
    kv_spec = pl.BlockSpec((tokens, kv_cols), lambda i, s: (0, 0))
    kv_weight = pl.BlockSpec((depth, kv_cols), lambda i, s: (s[0], 0))
    sums = [q_spec, kv_spec, kv_spec]
    return pl.pallas_call(
        project_kernel,
        grid_spec=pltpu.PrefetchScalarGridSpec(
            num_scalar_prefetch=1,
            grid=(query_cols // tile,),
            in_specs=[
                pl.BlockSpec((tokens, depth), lambda i, s: (0, 0)),
                pl.BlockSpec((depth, tile), lambda i, s: (s[0], i)),
                kv_weight,
                kv_weight,
            ]
            + (sums if carried else []),
            out_specs=sums,
        ),
        out_shape=[
            jax.ShapeDtypeStruct((tokens, cols), jnp.float32) for cols in (query_cols, kv_cols, kv_cols)
        ],
        compiler_params=pltpu.CompilerParams(vmem_limit_bytes=40 * 1024 * 1024),
        cost_estimate=pl.CostEstimate(
            flops=2 * tokens * depth * (query_cols + 2 * kv_cols),
            bytes_accessed=2 * depth * (query_cols + 2 * kv_cols) + 2 * tokens * depth,
            transcendentals=0,
        ),
    )(origin, rows, w_query, w_key, w_value, *carried)


def chunk_kernel(group, cache_tile, fresh, info, q_ref, k_ref, v_ref, *rest):
    head = pl.program_id(0)
    if fresh:
        nk_ref, nv_ref, acc_ref, stat_ref, s0, s1 = rest
    else:
        acc_ref, stat_ref, s0, s1 = rest
    tokens = q_ref.shape[0]
    cache_count = k_ref.shape[0]
    heads_tile = TILE_ROWS // tokens
    tiles = group // heads_tile
    half = stat_ref.shape[1] // 2
    scratch = (s0, s1)
    visible = info[1]
    spans = [(lo, min(cache_tile, cache_count - lo)) for lo in range(0, cache_count, cache_tile)]
    nt = (((1,), (1,)), ((), ()))

    def score(tile, buffer):
        queries = jnp.concatenate(
            [q_ref[:, pl.ds((tile * heads_tile + j) * HD, HD)] for j in range(heads_tile)], axis=0
        )
        best = jnp.full((TILE_ROWS, 128), MASK_FILL, jnp.float32)
        for lo, size in spans:
            raw = lax.dot_general(queries, k_ref[pl.ds(lo, size), :], nt, preferred_element_type=jnp.float32)
            place = lo + lax.broadcasted_iota(jnp.int32, (1, size), 1)
            raw = jnp.where(place < visible, raw, MASK_FILL)
            buffer[:, pl.ds(lo, size)] = raw
            for c in range(0, size, 128):
                best = jnp.maximum(best, raw[:, c : c + 128])
        if fresh:
            raw = lax.dot_general(queries, nk_ref[...], nt, preferred_element_type=jnp.float32)
            place = lax.broadcasted_iota(jnp.int32, (TILE_ROWS, tokens), 1)
            token = lax.broadcasted_iota(jnp.int32, (TILE_ROWS, tokens), 0) % tokens
            raw = jnp.where(place <= token, raw, MASK_FILL)
            buffer[:, pl.ds(cache_count, tokens)] = raw
            for c in range(0, tokens, 128):
                best = jnp.maximum(best, raw[:, c : c + 128])
        return jnp.max(best, axis=1, keepdims=True)

    lane = lax.broadcasted_iota(jnp.int32, (tokens, stat_ref.shape[1]), 1)

    def weigh(tile, buffer, top):
        shift = jnp.where(top > 0.5 * MASK_FILL, top, 0.0)
        total = jnp.zeros((TILE_ROWS, 2 * HD), jnp.float32)
        for lo, size in spans + ([(cache_count, tokens)] if fresh else []):
            weight = jnp.exp2(buffer[:, pl.ds(lo, size)] - shift).astype(jnp.bfloat16)
            value = v_ref[pl.ds(lo, size), :] if lo < cache_count else nv_ref[...]
            value = jnp.concatenate([value, jnp.ones((size, HD), jnp.bfloat16)], axis=1)
            total += jnp.dot(weight, value, preferred_element_type=jnp.float32)
        for j in range(heads_tile):
            index = tile * heads_tile + j
            rows = slice(j * tokens, (j + 1) * tokens)
            acc_ref[:, pl.ds(index * HD, HD)] = total[rows, :HD].astype(jnp.bfloat16)
            where = head * group + index
            stats = jnp.where(lane == where, jnp.broadcast_to(top[rows], lane.shape), stat_ref[...])
            stat_ref[...] = jnp.where(lane == half + where, total[rows, HD : HD + 1], stats)

    @pl.when(head == 0)
    def _():
        stat_ref[...] = jnp.zeros_like(stat_ref)

    top = score(0, scratch[0])
    for tile in range(tiles):
        later = score(tile + 1, scratch[(tile + 1) % 2]) if tile + 1 < tiles else None
        weigh(tile, scratch[tile % 2], top)
        top = later


def attend_chunk(info, queries, cache_k, cache_v, fresh, group):
    tokens, width = queries.shape
    kv_heads = width // HD // group
    cache_count = cache_k.shape[0]
    cache_spec = pl.BlockSpec((cache_count, HD), lambda g, s: (0, s[0] + g))
    new_spec = pl.BlockSpec((tokens, HD), lambda g, s: (0, g))
    return pl.pallas_call(
        functools.partial(chunk_kernel, group, min(1024, cache_count), bool(fresh)),
        grid_spec=pltpu.PrefetchScalarGridSpec(
            num_scalar_prefetch=1,
            grid=(kv_heads,),
            in_specs=[pl.BlockSpec((tokens, group * HD), lambda g, s: (0, g)), cache_spec, cache_spec]
            + [new_spec] * len(fresh),
            out_specs=[
                pl.BlockSpec((tokens, group * HD), lambda g, s: (0, g)),
                pl.BlockSpec((tokens, 128), lambda g, s: (0, 0)),
            ],
            scratch_shapes=[pltpu.VMEM((TILE_ROWS, cache_count + tokens), jnp.float32)] * 2,
        ),
        out_shape=[
            jax.ShapeDtypeStruct((tokens, width), jnp.bfloat16),
            jax.ShapeDtypeStruct((tokens, 128), jnp.float32),
        ],
        compiler_params=pltpu.CompilerParams(vmem_limit_bytes=48 * 1024 * 1024),
        cost_estimate=pl.CostEstimate(
            flops=8 * tokens * width * cache_count,
            bytes_accessed=4 * cache_count * kv_heads * HD + 4 * tokens * width,
            transcendentals=tokens * width // HD * cache_count,
        ),
    )(info, queries, cache_k, cache_v, *fresh)


def combine_kernel(parts, *refs):
    sums, stats, out_ref = refs[:parts], refs[parts : 2 * parts], refs[-1]
    heads = out_ref.shape[1] // HD
    half = stats[0].shape[1] // 2
    tops = [s[:, :half] for s in stats]
    top = functools.reduce(jnp.maximum, tops)
    factors = [jnp.exp2(t - top) for t in tops]
    total = sum(f * s[:, half:] for f, s in zip(factors, stats))
    for h in range(heads):
        number = sum(
            f[:, h : h + 1] * a[:, pl.ds(h * HD, HD)].astype(jnp.float32) for f, a in zip(factors, sums)
        )
        out_ref[:, pl.ds(h * HD, HD)] = (number / total[:, h : h + 1]).astype(jnp.bfloat16)


def combine(sums, stats):
    return pl.pallas_call(
        functools.partial(combine_kernel, len(sums)),
        out_shape=jax.ShapeDtypeStruct(sums[0].shape, jnp.bfloat16),
        compiler_params=pltpu.CompilerParams(vmem_limit_bytes=40 * 1024 * 1024),
    )(*sums, *stats)


def output_kernel(start, x_ref, w_ref, *rest):
    out_ref = rest[-1]
    projected = jnp.dot(x_ref[...], w_ref[...], preferred_element_type=jnp.float32)
    for c in range(0, out_ref.shape[1], QB):
        part = projected[:, c : c + QB]
        biggest = jnp.max(jnp.abs(part), axis=1, keepdims=True)
        scale = ((biggest + 1e-06) / 127.0).astype(jnp.bfloat16).astype(jnp.float32)
        value = (part / scale).astype(jnp.bfloat16).astype(jnp.float32) * scale
        for other in rest[:-1]:
            value += other[:, pl.ds(c, QB)].astype(jnp.float32)
        out_ref[:, pl.ds(c, QB)] = value.astype(jnp.bfloat16)


def output_part(owner, attended, w_out, others, feat_dev):
    tokens, depth = attended.shape
    tile = min(512, feat_dev)
    steps = feat_dev // tile
    spec = pl.BlockSpec((tokens, tile), lambda i, s: (0, i))
    return pl.pallas_call(
        output_kernel,
        grid_spec=pltpu.PrefetchScalarGridSpec(
            num_scalar_prefetch=1,
            grid=(steps,),
            in_specs=[
                pl.BlockSpec((tokens, depth), lambda i, s: (0, 0)),
                pl.BlockSpec((depth, tile), lambda i, s: (0, s[0] * steps + i)),
            ]
            + [spec] * len(others),
            out_specs=spec,
        ),
        out_shape=jax.ShapeDtypeStruct((tokens, feat_dev), jnp.bfloat16),
        compiler_params=pltpu.CompilerParams(vmem_limit_bytes=40 * 1024 * 1024),
        cost_estimate=pl.CostEstimate(
            flops=2 * tokens * depth * feat_dev,
            bytes_accessed=2 * depth * feat_dev + 4 * tokens * feat_dev,
            transcendentals=0,
        ),
    )(owner, attended, w_out, *others)


def on_device(
    hidden_states,
    norm_gain,
    w_query,
    b_query,
    w_key,
    b_key,
    w_value,
    b_value,
    w_out,
    cache_keys,
    cache_values,
    cached_lens,
    positions,
):
    devices = lax.axis_size("tensor")
    rank = lax.axis_index("tensor")
    tokens = hidden_states.shape[1]
    feat_dev = hidden_states.shape[2]
    blocks_dev = feat_dev // QB
    query_cols = w_query.shape[1]
    kv_cols = w_key.shape[1]
    cache_count = cache_keys.shape[1]

    def move(array, shift):
        return lax.ppermute(array, "tensor", [(i, (i + shift) % devices) for i in range(devices)])

    def index_of(shift):
        return ((rank + shift) % devices).astype(jnp.int32)

    local_rows = hidden_states[0].astype(jnp.float32)
    payload, block_scale = quantize(local_rows.reshape(tokens, blocks_dev, QB))
    restored = dequantize(payload, block_scale)
    gain_rows = norm_gain.reshape(1, blocks_dev, QB).astype(jnp.float32)
    held = (restored * gain_rows).astype(jnp.bfloat16).reshape(tokens, feat_dev)
    mine = jnp.sum(restored * restored, axis=(1, 2))
    squares = mine + sum(move(mine, shift) for shift in range(1, devices))
    sums = []
    for step in range(devices):
        arriving = move(held, 1) if step + 1 < devices else None
        sums = project_part(index_of(-step)[None], held, w_query, w_key, w_value, sums)
        held = arriving
    row_scale = lax.rsqrt(squares / (feat_dev * devices) + NORM_EPS)[:, None]
    cosine, sine = rotation_tables(positions[0])
    fold = LOG2E / math.sqrt(HD)
    query_full = row_scale * sums[0] + b_query.astype(jnp.float32)
    key_full = row_scale * sums[1] + b_key.astype(jnp.float32)
    query_rot = rotate_cols(
        query_full, fit_table(cosine * fold, 0, query_cols), fit_table(sine * fold, 0, query_cols)
    ).astype(jnp.bfloat16)
    key_rot = rotate_cols(
        key_full, fit_table(cosine, 0, kv_cols), fit_table(sine, 0, kv_cols)
    ).astype(jnp.bfloat16)
    value_new = (row_scale * sums[2] + b_value.astype(jnp.float32)).astype(jnp.bfloat16)

    visible = (cached_lens[0] - rank * cache_count).astype(jnp.int32)
    kv_dev = kv_cols // HD
    group = query_cols // kv_cols
    held = query_rot
    all_sums, all_stats = [], []
    for step in range(devices):
        arriving = move(held, -1) if step + 1 < devices else None
        info = jnp.stack([index_of(step) * kv_dev, visible])
        fresh = [key_rot, value_new] if step == 0 else []
        part, stat = attend_chunk(info, held, cache_keys[0], cache_values[0], fresh, group)
        all_sums.append(move(part, step) if step else part)
        all_stats.append(move(stat, step) if step else stat)
        held = arriving
    attended = combine(all_sums, all_stats)

    carried = []
    for step in range(1, devices):
        carried = [move(output_part(index_of(-step)[None], attended, w_out, carried, feat_dev), 1)]
    result = output_part(index_of(0)[None], attended, w_out, carried + [hidden_states[0]], feat_dev)
    return result[None]


def on_slice(*arrays):
    w_query, w_key = arrays[2], arrays[4]
    whole_heads = w_key.shape[1] % HD == 0 and w_query.shape[1] // HD <= 64
    return (on_device if whole_heads else on_device_split_heads)(*arrays)


def solution(mesh):
    return jax.shard_map(
        on_slice,
        mesh=mesh,
        in_specs=(
            P(("groups", "dp"), None, "tensor"),
            P("tensor"),
            P(None, "tensor"),
            P("tensor"),
            P(None, "tensor"),
            P("tensor"),
            P(None, "tensor"),
            P("tensor"),
            P("tensor", None),
            P(("groups", "dp"), "tensor", None),
            P(("groups", "dp"), "tensor", None),
            P(("groups", "dp")),
            P(("groups", "dp"), None),
        ),
        out_specs=P(("groups", "dp"), None, "tensor"),
        check_vma=False,
    )
```

```python
import functools
import math

import jax
import jax.numpy as jnp
from jax import lax
from jax.experimental import pallas as pl
from jax.experimental.pallas import tpu as pltpu
from jax.sharding import PartitionSpec as P

HD = 128
QB = 128


ROPE_BASE = 1000000.0
NORM_EPS = 1e-06
MASK_FILL = -1e30
LOG2E = 1.4426950408889634
TILE_ROWS = 256


def quantize(values):
    biggest = jnp.max(jnp.abs(values), axis=-1)
    block_scale = ((biggest + 1e-06) / 127.0).astype(jnp.bfloat16)
    payload = (values / block_scale.astype(jnp.float32)[..., None]).astype(jnp.bfloat16)
    return (payload, block_scale)


def dequantize(payload, block_scale):
    return payload.astype(jnp.float32) * block_scale.astype(jnp.float32)[..., None]


def rotation_tables(token_pos):
    column = jnp.arange(HD, dtype=jnp.int32)
    pair_index = column // 2
    inverse = jnp.power(ROPE_BASE, -2.0 * pair_index.astype(jnp.float32) / HD)
    angles = token_pos.astype(jnp.float32)[:, None] * inverse[None, :]
    sign = jnp.where(column % 2 == 0, -1.0, 1.0)
    return jnp.cos(angles), jnp.sin(angles) * sign[None, :]


def fit_table(table, first_col, cols):
    if cols >= HD:
        return jnp.tile(table, (1, cols // HD))
    return lax.dynamic_slice_in_dim(table, first_col % HD, cols, 1)


def rotate_cols(values, cosine, sine):
    even = jnp.arange(values.shape[1], dtype=jnp.int32) % 2 == 0
    swapped = jnp.where(even[None, :], jnp.roll(values, -1, axis=1), jnp.roll(values, 1, axis=1))
    return values * cosine + swapped * sine


def attend_kernel(group, cache_tile, info, q_ref, k_ref, v_ref, nk_ref, nv_ref, acc_ref, stat_ref, s0, s1):
    head = pl.program_id(0)
    tokens = q_ref.shape[0]
    cache_count = k_ref.shape[0]
    new_count = nk_ref.shape[0]
    heads_tile = TILE_ROWS // tokens
    tiles = group // heads_tile
    head_count = group * pl.num_programs(0)
    scratch = (s0, s1)
    visible, new_first, new_valid = info[0], info[1], info[2]
    spans = [(lo, min(cache_tile, cache_count - lo)) for lo in range(0, cache_count, cache_tile)]
    nt = (((1,), (1,)), ((), ()))

    def score(tile, buffer):
        queries = jnp.concatenate(
            [q_ref[:, pl.ds((tile * heads_tile + j) * HD, HD)] for j in range(heads_tile)], axis=0
        )
        best = jnp.full((TILE_ROWS, 128), MASK_FILL, jnp.float32)
        for lo, size in spans:
            raw = lax.dot_general(queries, k_ref[pl.ds(lo, size), :], nt, preferred_element_type=jnp.float32)
            place = lo + lax.broadcasted_iota(jnp.int32, (1, size), 1)
            raw = jnp.where(place < visible, raw, MASK_FILL)
            buffer[:, pl.ds(lo, size)] = raw
            for c in range(0, size, 128):
                best = jnp.maximum(best, raw[:, c : c + 128])
        raw = lax.dot_general(queries, nk_ref[...], nt, preferred_element_type=jnp.float32)
        place = lax.broadcasted_iota(jnp.int32, (TILE_ROWS, new_count), 1)
        token = lax.broadcasted_iota(jnp.int32, (TILE_ROWS, new_count), 0) % tokens
        raw = jnp.where((place < new_valid) & (new_first + place <= token), raw, MASK_FILL)
        buffer[:, pl.ds(cache_count, new_count)] = raw
        for c in range(0, new_count, 128):
            best = jnp.maximum(best, raw[:, c : c + 128])
        return jnp.max(best, axis=1, keepdims=True)

    lane = lax.broadcasted_iota(jnp.int32, (tokens, stat_ref.shape[1]), 1)

    def weigh(tile, buffer, top):
        shift = jnp.where(top > 0.5 * MASK_FILL, top, 0.0)
        total = jnp.zeros((TILE_ROWS, 2 * HD), jnp.float32)
        for lo, size in spans + [(cache_count, new_count)]:
            weight = jnp.exp2(buffer[:, pl.ds(lo, size)] - shift).astype(jnp.bfloat16)
            value = v_ref[pl.ds(lo, size), :] if lo < cache_count else nv_ref[...]
            value = jnp.concatenate([value, jnp.ones((size, HD), jnp.bfloat16)], axis=1)
            total += jnp.dot(weight, value, preferred_element_type=jnp.float32)
        for j in range(heads_tile):
            index = tile * heads_tile + j
            rows = slice(j * tokens, (j + 1) * tokens)
            acc_ref[:, pl.ds(index * HD, HD)] = total[rows, :HD].astype(jnp.bfloat16)
            where = head * group + index
            stats = jnp.where(lane == where, jnp.broadcast_to(top[rows], lane.shape), stat_ref[...])
            stat_ref[...] = jnp.where(lane == head_count + where, total[rows, HD : HD + 1], stats)

    @pl.when(head == 0)
    def _():
        stat_ref[...] = jnp.zeros_like(stat_ref)

    top = score(0, scratch[0])
    for tile in range(tiles):
        later = score(tile + 1, scratch[(tile + 1) % 2]) if tile + 1 < tiles else None
        weigh(tile, scratch[tile % 2], top)
        top = later


def attend(queries, cache_k, cache_v, new_k, new_v, info, kv_heads):
    tokens, width = queries.shape
    group = width // HD // kv_heads
    cache_count = cache_k.shape[0]
    new_count = new_k.shape[0]
    return pl.pallas_call(
        functools.partial(attend_kernel, group, min(1024, cache_count)),
        grid=(kv_heads,),
        in_specs=[
            pl.BlockSpec(memory_space=pltpu.SMEM),
            pl.BlockSpec((tokens, group * HD), lambda g: (0, g)),
            pl.BlockSpec((cache_count, HD), lambda g: (0, g)),
            pl.BlockSpec((cache_count, HD), lambda g: (0, g)),
            pl.BlockSpec((new_count, HD), lambda g: (0, g)),
            pl.BlockSpec((new_count, HD), lambda g: (0, g)),
        ],
        out_specs=[
            pl.BlockSpec((tokens, group * HD), lambda g: (0, g)),
            pl.BlockSpec((tokens, 2 * width // HD), lambda g: (0, 0)),
        ],
        out_shape=[
            jax.ShapeDtypeStruct((tokens, width), jnp.bfloat16),
            jax.ShapeDtypeStruct((tokens, 2 * width // HD), jnp.float32),
        ],
        scratch_shapes=[pltpu.VMEM((TILE_ROWS, cache_count + new_count), jnp.float32)] * 2,
        compiler_params=pltpu.CompilerParams(vmem_limit_bytes=48 * 1024 * 1024),
        cost_estimate=pl.CostEstimate(
            flops=4 * tokens * width * (cache_count + new_count),
            bytes_accessed=4 * cache_count * kv_heads * HD + 4 * tokens * width,
            transcendentals=tokens * width // HD * (cache_count + new_count),
        ),
    )(info, queries, cache_k, cache_v, new_k, new_v)


def on_device_split_heads(
    hidden_states,
    norm_gain,
    w_query,
    b_query,
    w_key,
    b_key,
    w_value,
    b_value,
    w_out,
    cache_keys,
    cache_values,
    cached_lens,
    positions,
):
    devices = lax.axis_size("tensor")
    tensor_rank = lax.axis_index("tensor")
    tokens = hidden_states.shape[1]
    feat_dev = hidden_states.shape[2]
    blocks_dev = feat_dev // QB
    full_width = feat_dev * devices
    query_cols = w_query.shape[1]
    kv_cols = w_key.shape[1]
    local_rows = hidden_states[0].astype(jnp.float32)
    payload, block_scale = quantize(local_rows.reshape(tokens, blocks_dev, QB))
    restored = dequantize(payload, block_scale)
    gain_rows = norm_gain.reshape(1, blocks_dev, QB).astype(jnp.float32)
    scaled_dev = (restored * gain_rows).astype(jnp.bfloat16).reshape(tokens, feat_dev)
    squares = lax.psum(jnp.sum(restored * restored, axis=(1, 2)), "tensor")
    scaled = lax.all_gather(scaled_dev, "tensor", axis=1, tiled=True)
    query_acc = jnp.dot(scaled, w_query, preferred_element_type=jnp.float32)
    key_acc = jnp.dot(scaled, w_key, preferred_element_type=jnp.float32)
    value_acc = jnp.dot(scaled, w_value, preferred_element_type=jnp.float32)
    inv_rms = lax.rsqrt(squares / full_width + NORM_EPS)
    row_scale = inv_rms[:, None]
    cosine, sine = rotation_tables(positions[0])
    query_full = row_scale * query_acc + b_query.astype(jnp.float32)
    key_full = row_scale * key_acc + b_key.astype(jnp.float32)
    fold = LOG2E / math.sqrt(HD)
    query_rot = rotate_cols(
        query_full,
        fit_table(cosine * fold, tensor_rank * query_cols, query_cols),
        fit_table(sine * fold, tensor_rank * query_cols, query_cols),
    ).astype(jnp.bfloat16)
    key_rot = rotate_cols(
        key_full,
        fit_table(cosine, tensor_rank * kv_cols, kv_cols),
        fit_table(sine, tensor_rank * kv_cols, kv_cols),
    ).astype(jnp.bfloat16)
    value_new = (row_scale * value_acc + b_value.astype(jnp.float32)).astype(jnp.bfloat16)
    cache_count = cache_keys.shape[1]
    per_dev = query_cols // HD
    block_keys, block_values = (
        lax.all_to_all(key_rot, "tensor", split_axis=0, concat_axis=1, tiled=True),
        lax.all_to_all(value_new, "tensor", split_axis=0, concat_axis=1, tiled=True),
    )
    all_queries = lax.all_gather(query_rot, "tensor", axis=1, tiled=True)
    kv_heads = block_keys.shape[1] // HD
    new_count = block_keys.shape[0]
    pad = -new_count % 128
    info = jnp.stack(
        [cached_lens[0] - tensor_rank * cache_count, tensor_rank * new_count, jnp.int32(new_count)]
    ).astype(jnp.int32)
    sums, stats = attend(
        all_queries,
        cache_keys[0],
        cache_values[0],
        jnp.pad(block_keys, ((0, pad), (0, 0))),
        jnp.pad(block_values, ((0, pad), (0, 0))),
        info,
        kv_heads,
    )
    acc_in = lax.all_to_all(
        sums.reshape(tokens, devices, per_dev * HD), "tensor", split_axis=1, concat_axis=1, tiled=True
    )
    stat_in = lax.all_to_all(
        stats.reshape(tokens, 2, devices, per_dev), "tensor", split_axis=2, concat_axis=2, tiled=True
    )
    max_in, tot_in = stat_in[:, 0], stat_in[:, 1]
    top_max = jnp.max(max_in, axis=1, keepdims=True)
    factor = jnp.exp2(max_in - top_max)
    numerator = jnp.sum(
        acc_in.astype(jnp.float32).reshape(tokens, devices, per_dev, HD) * factor[..., None], axis=1
    )
    denominator = jnp.sum(factor * tot_in, axis=1)
    attended = (
        (numerator / denominator[..., None]).astype(jnp.bfloat16).reshape(tokens, per_dev * HD)
    )
    projected = jnp.dot(attended, w_out, preferred_element_type=jnp.float32)
    out_pay, out_scale = quantize(projected.reshape(tokens, full_width // QB, QB))
    recv_pay, recv_scale = (
        lax.all_to_all(out_pay, "tensor", split_axis=1, concat_axis=0, tiled=True),
        lax.all_to_all(out_scale, "tensor", split_axis=1, concat_axis=0, tiled=True),
    )
    summed_in = jnp.sum(
        dequantize(recv_pay, recv_scale).reshape(devices, tokens, blocks_dev, QB), axis=0
    )
    result = (local_rows + summed_in.reshape(tokens, feat_dev)).astype(jnp.bfloat16)
    return result[None]


def project_kernel(start, x_ref, wq_ref, wk_ref, wv_ref, *rest):
    carried, (q_out, k_out, v_out) = rest[:-3], rest[-3:]
    rows = x_ref[...]

    def step(weight, place):
        term = jnp.dot(rows, weight[...], preferred_element_type=jnp.float32)
        return term + carried[place][...] if carried else term

    q_out[...] = step(wq_ref, 0)

    @pl.when(pl.program_id(0) == 0)
    def _():
        k_out[...] = step(wk_ref, 1)
        v_out[...] = step(wv_ref, 2)


def project_part(rank, shift, rows, w_query, w_key, w_value, carried):
    tokens, depth = rows.shape
    query_cols, kv_cols = w_query.shape[1], w_key.shape[1]
    tile = min(512, query_cols)
    q_spec = pl.BlockSpec((tokens, tile), lambda i, s: (0, i))
    kv_spec = pl.BlockSpec((tokens, kv_cols), lambda i, s: (0, 0))
    devices = w_query.shape[0] // depth
    kv_weight = pl.BlockSpec((depth, kv_cols), lambda i, s: (lax.rem(s[0] + shift, devices), 0))
    sums = [q_spec, kv_spec, kv_spec]
    return pl.pallas_call(
        project_kernel,
        grid_spec=pltpu.PrefetchScalarGridSpec(
            num_scalar_prefetch=1,
            grid=(query_cols // tile,),
            in_specs=[
                pl.BlockSpec((tokens, depth), lambda i, s: (0, 0)),
                pl.BlockSpec((depth, tile), lambda i, s: (lax.rem(s[0] + shift, devices), i)),
                kv_weight,
                kv_weight,
            ]
            + (sums if carried else []),
            out_specs=sums,
        ),
        out_shape=[
            jax.ShapeDtypeStruct((tokens, cols), jnp.float32) for cols in (query_cols, kv_cols, kv_cols)
        ],
        compiler_params=pltpu.CompilerParams(vmem_limit_bytes=40 * 1024 * 1024),
        cost_estimate=pl.CostEstimate(
            flops=2 * tokens * depth * (query_cols + 2 * kv_cols),
            bytes_accessed=2 * depth * (query_cols + 2 * kv_cols) + 2 * tokens * depth,
            transcendentals=0,
        ),
    )(rank, rows, w_query, w_key, w_value, *carried)


def chunk_kernel(group, cache_tile, fresh, first, info, q_ref, k_ref, v_ref, *rest):
    head = pl.program_id(0)
    if fresh:
        nk_ref, nv_ref, acc_ref, stat_ref, s0, s1 = rest
    else:
        acc_ref, stat_ref, s0, s1 = rest
    tokens = q_ref.shape[0]
    cache_count = k_ref.shape[0]
    heads_tile = TILE_ROWS // tokens
    tiles = group // heads_tile
    half = stat_ref.shape[1] // 2
    scratch = (s0, s1)
    visible = info[1]
    spans = [(lo, min(cache_tile, cache_count - lo)) for lo in range(0, cache_count, cache_tile)]
    nt = (((1,), (1,)), ((), ()))

    def score(tile, buffer):
        queries = jnp.concatenate(
            [q_ref[:, pl.ds((tile * heads_tile + j) * HD, HD)] for j in range(heads_tile)], axis=0
        )
        best = jnp.full((TILE_ROWS, 128), MASK_FILL, jnp.float32)
        for lo, size in spans:
            raw = lax.dot_general(queries, k_ref[pl.ds(lo, size), :], nt, preferred_element_type=jnp.float32)
            place = lo + lax.broadcasted_iota(jnp.int32, (1, size), 1)
            raw = jnp.where(place < visible, raw, MASK_FILL)
            buffer[:, pl.ds(lo, size)] = raw
            for c in range(0, size, 128):
                best = jnp.maximum(best, raw[:, c : c + 128])
        if fresh:
            raw = lax.dot_general(queries, nk_ref[...], nt, preferred_element_type=jnp.float32)
            place = lax.broadcasted_iota(jnp.int32, (TILE_ROWS, tokens), 1)
            token = lax.broadcasted_iota(jnp.int32, (TILE_ROWS, tokens), 0) % tokens
            raw = jnp.where(place <= token, raw, MASK_FILL)
            buffer[:, pl.ds(cache_count, tokens)] = raw
            for c in range(0, tokens, 128):
                best = jnp.maximum(best, raw[:, c : c + 128])
        return jnp.max(best, axis=1, keepdims=True)

    lane = lax.broadcasted_iota(jnp.int32, (tokens, stat_ref.shape[1]), 1)

    def weigh(tile, buffer, top):
        shift = jnp.where(top > 0.5 * MASK_FILL, top, 0.0)
        total = jnp.zeros((TILE_ROWS, 2 * HD), jnp.float32)
        for lo, size in spans + ([(cache_count, tokens)] if fresh else []):
            weight = jnp.exp2(buffer[:, pl.ds(lo, size)] - shift).astype(jnp.bfloat16)
            value = v_ref[pl.ds(lo, size), :] if lo < cache_count else nv_ref[...]
            value = jnp.concatenate([value, jnp.ones((size, HD), jnp.bfloat16)], axis=1)
            total += jnp.dot(weight, value, preferred_element_type=jnp.float32)
        for j in range(heads_tile):
            index = tile * heads_tile + j
            rows = slice(j * tokens, (j + 1) * tokens)
            acc_ref[:, pl.ds(index * HD, HD)] = total[rows, :HD].astype(jnp.bfloat16)
            where = (first + head) * group + index
            stats = jnp.where(lane == where, jnp.broadcast_to(top[rows], lane.shape), stat_ref[...])
            stat_ref[...] = jnp.where(lane == half + where, total[rows, HD : HD + 1], stats)

    @pl.when(head == 0)
    def _():
        stat_ref[...] = jnp.zeros_like(stat_ref)

    top = score(0, scratch[0])
    for tile in range(tiles):
        later = score(tile + 1, scratch[(tile + 1) % 2]) if tile + 1 < tiles else None
        weigh(tile, scratch[tile % 2], top)
        top = later


def attend_chunk(info, shift, first, kv_heads, kv_dev, queries, cache_k, cache_v, fresh, group):
    tokens = queries.shape[0]
    width = kv_heads * group * HD
    cache_count = cache_k.shape[0]
    devices = cache_k.shape[1] // (kv_dev * HD)
    cache_spec = pl.BlockSpec(
        (cache_count, HD), lambda g, s: (0, lax.rem(s[0] + shift, devices) * kv_dev + first + g)
    )
    new_spec = pl.BlockSpec((tokens, HD), lambda g, s: (0, first + g))
    return pl.pallas_call(
        functools.partial(chunk_kernel, group, min(1024, cache_count), bool(fresh), first),
        grid_spec=pltpu.PrefetchScalarGridSpec(
            num_scalar_prefetch=1,
            grid=(kv_heads,),
            in_specs=[pl.BlockSpec((tokens, group * HD), lambda g, s: (0, first + g)), cache_spec, cache_spec]
            + [new_spec] * len(fresh),
            out_specs=[
                pl.BlockSpec((tokens, group * HD), lambda g, s: (0, g)),
                pl.BlockSpec((tokens, 128), lambda g, s: (0, 0)),
            ],
            scratch_shapes=[pltpu.VMEM((TILE_ROWS, cache_count + tokens), jnp.float32)] * 2,
        ),
        out_shape=[
            jax.ShapeDtypeStruct((tokens, width), jnp.bfloat16),
            jax.ShapeDtypeStruct((tokens, 128), jnp.float32),
        ],
        compiler_params=pltpu.CompilerParams(vmem_limit_bytes=48 * 1024 * 1024),
        cost_estimate=pl.CostEstimate(
            flops=8 * tokens * width * cache_count,
            bytes_accessed=4 * cache_count * kv_heads * HD + 4 * tokens * width,
            transcendentals=tokens * width // HD * cache_count,
        ),
    )(info, queries, cache_k, cache_v, *fresh)


def combine_kernel(parts, *refs):
    sums, stats, out_ref = refs[:parts], refs[parts : 2 * parts], refs[-1]
    heads = out_ref.shape[1] // HD
    half = stats[0].shape[1] // 2
    tops = [s[:, :half] for s in stats]
    top = functools.reduce(jnp.maximum, tops)
    factors = [jnp.exp2(t - top) for t in tops]
    total = sum(f * s[:, half:] for f, s in zip(factors, stats))
    for h in range(heads):
        number = sum(
            f[:, h : h + 1] * a[:, pl.ds(h * HD, HD)].astype(jnp.float32) for f, a in zip(factors, sums)
        )
        out_ref[:, pl.ds(h * HD, HD)] = (number / total[:, h : h + 1]).astype(jnp.bfloat16)


def combine(sums, stats):
    return pl.pallas_call(
        functools.partial(combine_kernel, len(sums)),
        out_shape=jax.ShapeDtypeStruct(sums[0].shape, jnp.bfloat16),
        compiler_params=pltpu.CompilerParams(vmem_limit_bytes=40 * 1024 * 1024),
    )(*sums, *stats)


def output_kernel(start, x_ref, w_ref, *rest):
    out_ref = rest[-1]
    projected = jnp.dot(x_ref[...], w_ref[...], preferred_element_type=jnp.float32)
    for c in range(0, out_ref.shape[1], QB):
        part = projected[:, c : c + QB]
        biggest = jnp.max(jnp.abs(part), axis=1, keepdims=True)
        scale = ((biggest + 1e-06) / 127.0).astype(jnp.bfloat16).astype(jnp.float32)
        value = (part / scale).astype(jnp.bfloat16).astype(jnp.float32) * scale
        for other in rest[:-1]:
            value += other[:, pl.ds(c, QB)].astype(jnp.float32)
        out_ref[:, pl.ds(c, QB)] = value.astype(jnp.bfloat16)


def output_part(rank, shift, half, halves, attended, w_out, others, feat_dev):
    tokens, depth = attended.shape
    devices = w_out.shape[1] // feat_dev
    part_cols = feat_dev // halves
    tile = min(512, part_cols)
    steps = part_cols // tile
    spec = pl.BlockSpec((tokens, tile), lambda i, s: (0, i))
    return pl.pallas_call(
        output_kernel,
        grid_spec=pltpu.PrefetchScalarGridSpec(
            num_scalar_prefetch=1,
            grid=(steps,),
            in_specs=[
                pl.BlockSpec((tokens, depth), lambda i, s: (0, 0)),
                pl.BlockSpec(
                    (depth, tile),
                    lambda i, s: (0, (lax.rem(s[0] + shift, devices) * halves + half) * steps + i),
                ),
            ]
            + [spec] * len(others),
            out_specs=spec,
        ),
        out_shape=jax.ShapeDtypeStruct((tokens, part_cols), jnp.bfloat16),
        compiler_params=pltpu.CompilerParams(vmem_limit_bytes=40 * 1024 * 1024),
        cost_estimate=pl.CostEstimate(
            flops=2 * tokens * depth * part_cols,
            bytes_accessed=2 * depth * part_cols + 4 * tokens * part_cols,
            transcendentals=0,
        ),
    )(rank, attended, w_out, *others)


def on_device(
    hidden_states,
    norm_gain,
    w_query,
    b_query,
    w_key,
    b_key,
    w_value,
    b_value,
    w_out,
    cache_keys,
    cache_values,
    cached_lens,
    positions,
):
    devices = lax.axis_size("tensor")
    rank = lax.axis_index("tensor")
    tokens = hidden_states.shape[1]
    feat_dev = hidden_states.shape[2]
    blocks_dev = feat_dev // QB
    query_cols = w_query.shape[1]
    kv_cols = w_key.shape[1]
    cache_count = cache_keys.shape[1]

    def move(array, shift):
        return lax.ppermute(array, "tensor", [(i, (i + shift) % devices) for i in range(devices)])

    place = jnp.stack([rank, cached_lens[0] - rank * cache_count]).astype(jnp.int32)

    local_rows = hidden_states[0].astype(jnp.float32)
    payload, block_scale = quantize(local_rows.reshape(tokens, blocks_dev, QB))
    restored = dequantize(payload, block_scale)
    gain_rows = norm_gain.reshape(1, blocks_dev, QB).astype(jnp.float32)
    held = (restored * gain_rows).astype(jnp.bfloat16).reshape(tokens, feat_dev)
    mine = jnp.sum(restored * restored, axis=(1, 2))
    squares = mine + sum(move(mine, shift) for shift in range(1, devices))
    sums = []
    for step in range(devices):
        arriving = move(held, 1) if step + 1 < devices else None
        sums = project_part(place[:1], devices - step, held, w_query, w_key, w_value, sums)
        if step + 1 < devices:
            held, *sums = lax.optimization_barrier((arriving, *sums))
    row_scale = lax.rsqrt(squares / (feat_dev * devices) + NORM_EPS)[:, None]
    cosine, sine = rotation_tables(positions[0])
    fold = LOG2E / math.sqrt(HD)
    query_full = row_scale * sums[0] + b_query.astype(jnp.float32)
    key_full = row_scale * sums[1] + b_key.astype(jnp.float32)
    query_rot = rotate_cols(
        query_full, fit_table(cosine * fold, 0, query_cols), fit_table(sine * fold, 0, query_cols)
    ).astype(jnp.bfloat16)
    key_rot = rotate_cols(
        key_full, fit_table(cosine, 0, kv_cols), fit_table(sine, 0, kv_cols)
    ).astype(jnp.bfloat16)
    value_new = (row_scale * sums[2] + b_value.astype(jnp.float32)).astype(jnp.bfloat16)

    group = query_cols // kv_cols
    kv_dev = kv_cols // HD
    lead = kv_dev // 2
    cache = (cache_keys[0], cache_values[0])
    arriving = move(query_rot, -1)
    own_lead = attend_chunk(place, 0, 0, lead, kv_dev, query_rot, *cache, [key_rot, value_new], group)
    held, *own_lead = lax.optimization_barrier((arriving, *own_lead))
    all_sums, all_stats = [], []
    for step in range(1, devices):
        arriving = move(held, -1) if step + 1 < devices else None
        part, stat = attend_chunk(place, step, 0, kv_dev, kv_dev, held, *cache, [], group)
        if step + 1 == devices:
            part, stat, key_rot = lax.optimization_barrier((part, stat, key_rot))
        all_sums.append(move(part, step))
        all_stats.append(move(stat, step))
        held = arriving
    own_rest = attend_chunk(
        place, 0, lead, kv_dev - lead, kv_dev, query_rot, *cache, [key_rot, value_new], group
    )
    all_sums.append(jnp.concatenate([own_lead[0], own_rest[0]], axis=1))
    all_stats.append(own_lead[1] + own_rest[1])
    attended = combine(all_sums, all_stats)

    halves = 2
    carried = [[]] * halves
    for step in range(1, devices):
        carried = [
            [move(output_part(place[:1], devices - step, h, halves, attended, w_out, carried[h], feat_dev), 1)]
            for h in range(halves)
        ]
    cols = feat_dev // halves
    result = jnp.concatenate(
        [
            output_part(
                place[:1],
                0,
                h,
                halves,
                attended,
                w_out,
                carried[h] + [hidden_states[0][:, h * cols : (h + 1) * cols]],
                feat_dev,
            )
            for h in range(halves)
        ],
        axis=1,
    )
    return result[None]


def on_slice(*arrays):
    w_query, w_key = arrays[2], arrays[4]
    whole_heads = w_key.shape[1] % (2 * HD) == 0 and w_query.shape[1] // HD <= 64
    return (on_device if whole_heads else on_device_split_heads)(*arrays)


def solution(mesh):
    return jax.shard_map(
        on_slice,
        mesh=mesh,
        in_specs=(
            P(("groups", "dp"), None, "tensor"),
            P("tensor"),
            P(None, "tensor"),
            P("tensor"),
            P(None, "tensor"),
            P("tensor"),
            P(None, "tensor"),
            P("tensor"),
            P("tensor", None),
            P(("groups", "dp"), "tensor", None),
            P(("groups", "dp"), "tensor", None),
            P(("groups", "dp")),
            P(("groups", "dp"), None),
        ),
        out_specs=P(("groups", "dp"), None, "tensor"),
        check_vma=False,
    )
```
